512 devices in a mesh: dp: 8 (over y_hi, core), fsdp: 64 (over y_lo, x, z).
Axes of the slice: x: 4, y: 8 (y_hi: 4, y_lo: 2; y = y_hi * 2 + y_lo), z: 8, core: 2. Of those that a mesh axis runs over, the one named last changes fastest.
Arguments:
- residual: bfloat16 [131072, 3200], P(('dp', 'fsdp')), may hold values from -6 to 6
- heads_out: bfloat16 [131072, 2048], P(('dp', 'fsdp')), may hold values from -6 to 6
- out_weight: bfloat16 [2048, 3200], P(('dp', 'fsdp')), may hold values from -0.125 to 0.125
- out_bias: float32 [3200], replicated, may hold values from -3 to 3
- layer_scale: float32 [3200], replicated, may hold values from 0.3 to 3
Outputs:
- updated: bfloat16 [131072, 3200], P(('dp', 'fsdp'))
The draws below stay inside these ranges and needn't reach their ends.
All inputs are finite; a program needn't handle non-finite values.
Results may differ from the reference program's by a relative error of at most 0.001.
Values may be sent and summed in bfloat16 or wider, within the bound.
No kernel may reach another device: no remote copies, remote signals or barrier semaphores. Data moves between devices by JAX's collectives and lax.ppermute only.
A program may use at most 128 MiB of HBM per device.

```python
import math
import jax
import jax.numpy as jnp
from jax import lax

D = 3200
TOK_DEV = 256
TOKENS = 131072
INNER = 2048


def block_scale(stream_key, extent, split, smallest, largest):
    factor_of = 1.0
    for position, shards_of in split:
        heights = jax.random.uniform(jax.random.fold_in(jax.random.fold_in(stream_key, 6), position), (shards_of,), jnp.float32, smallest / len(split), largest / len(split))
        factor_of = factor_of * jnp.repeat(jnp.exp(heights), extent[position] // shards_of).reshape((-1,) + (1,) * (len(extent) - 1 - position))
    return factor_of


def bell_draw(rng, extent, deviation, limit, pieces=(), dtype=jnp.bfloat16):
    gain = block_scale(rng, extent, pieces, -0.22, 0.18) if pieces else 1.0
    result = jax.random.normal(rng, extent, jnp.float32) * deviation * gain
    return jnp.minimum(jnp.maximum(result, -limit), limit).astype(dtype)


def setup_inputs(seed: int = 0) -> dict:
    splits = jax.random.split(jax.random.key(seed), 6)
    return {
        "residual": bell_draw(splits[0], (TOKENS, D), 1.0, 6.0, ((0, 512),)),
        "heads_out": bell_draw(splits[1], (TOKENS, INNER), 1.0, 6.0, ((0, 512),)),
        "out_weight": bell_draw(splits[2], (INNER, D), INNER ** -0.5, 0.125, ((0, 512),)),
        "out_bias": bell_draw(splits[3], (D,), 0.5, 3.0, (), jnp.float32),
        "layer_scale": jnp.clip(jnp.exp(jax.random.uniform(splits[4], (D,), jnp.float32, math.log(0.3), math.log(3.0))), 0.3, 3.0),
    }


def reference(residual, heads_out, out_weight, out_bias, layer_scale):
    weight_full = out_weight.astype(jnp.float32)

    def encode_block(block_pair):
        stream_rows, head_rows = block_pair
        projected = jnp.dot(head_rows.astype(jnp.float32), weight_full, preferred_element_type=jnp.float32)
        branch = layer_scale * (projected + out_bias)
        return (stream_rows.astype(jnp.float32) + branch).astype(jnp.bfloat16)

    stream_blocks = residual.reshape(TOKENS // TOK_DEV, TOK_DEV, D)
    head_blocks = heads_out.reshape(TOKENS // TOK_DEV, TOK_DEV, INNER)
    updated = lax.map(encode_block, (stream_blocks, head_blocks))
    return updated.reshape(TOKENS, D)
```

```python
import jax
import jax.numpy as jnp
import numpy as np
from jax import lax
from jax.sharding import Mesh, PartitionSpec as P

D = 3200
WIDE = 1664
SKIP = D - WIDE
Y, CORES, X, Z = 8, 2, 4, 8
DEVICES = Y * CORES * X * Z
CLASSES = 8
ROWS = 4
DEPTH = DEVICES * ROWS // CLASSES


def index_of(core, x, y, z):
    y, x, z = y % Y, x % X, z % Z
    return (((y // 2 * CORES + core) * 2 + y % 2) * X + x) * Z + z


def places():
    for core in range(CORES):
        for x in range(X):
            for y in range(Y):
                for z in range(Z):
                    yield core, x, y, z


def class_of(x, y, z):
    return (2 * x + y + 3 * z) % CLASSES


def class_groups():
    groups = [[] for _ in range(CLASSES)]
    for core, x, y, z in places():
        groups[class_of(x, y, z)].append(index_of(core, x, y, z))
    return [sorted(g) for g in groups]


def shift(dx, dy, dz, dx1=None, dy1=None, dz1=None):
    if dx1 is None:
        dx1, dy1, dz1 = dx, dy, dz
    pairs = []
    for core, x, y, z in places():
        ex, ey, ez = (dx, dy, dz) if core == 0 else (dx1, dy1, dz1)
        pairs.append((index_of(core, x, y, z), index_of(core, x + ex, y + ey, z + ez)))
    return pairs


OTHER_CORE = [(index_of(c, x, y, z), index_of(1 - c, x, y, z)) for c, x, y, z in places()]
GROUPS = class_groups()
ORDER = np.array([d * ROWS + i for g in GROUPS for d in g for i in range(ROWS)])
MOVES = [
    (shift(0, 1, 1, 0, -1, -1), 4),
    (shift(0, 1, 0), -1),
    (shift(0, -1, 0), 1),
    (shift(0, 0, 1), -3),
    (shift(0, 0, -1), 3),
    (shift(1, 0, 0), -2),
    (shift(-1, 0, 0), 2),
]


def body(residual, heads_out, out_weight, out_bias, layer_scale):
    me = lax.axis_index("d")
    core = me // (2 * X * Z) % CORES
    z = me % Z
    x = me // Z % X
    y = me // (CORES * 2 * X * Z) * 2 + me // (X * Z) % 2
    mine = (2 * x + y + 3 * z) % CLASSES
    first = core * SKIP

    halves = jnp.stack([out_weight[:, :WIDE], out_weight[:, SKIP:]])
    cores = np.array([g // (2 * X * Z) % CORES for g in GROUPS[0]])
    for_each = halves[cores]
    block = lax.all_to_all(for_each, "d", 0, 0, axis_index_groups=GROUPS, tiled=True)
    block = block.reshape(DEPTH, WIDE)
    blocks = [block] + [lax.ppermute(block, "d", pairs) for pairs, _ in MOVES]

    pick = (lax.broadcasted_iota(jnp.int32, (2048, 2048), 0) == ORDER.astype(np.int32)[None, :]).astype(jnp.bfloat16)
    own_heads = jnp.dot(heads_out, pick, preferred_element_type=jnp.float32).astype(jnp.bfloat16)
    heads = jnp.stack([own_heads, lax.ppermute(own_heads, "d", OTHER_CORE)])
    own_part = lax.dynamic_slice_in_dim(residual, first, WIDE, 1)
    other_part = lax.dynamic_slice_in_dim(residual, SKIP - first, WIDE, 1)
    came = lax.ppermute(other_part, "d", OTHER_CORE)
    stream = jnp.stack([own_part, came])
    scale = lax.dynamic_slice_in_dim(layer_scale, first, WIDE, 0)
    bias = lax.dynamic_slice_in_dim(out_bias, first, WIDE, 0)

    total = 0.0
    for part, more in zip(blocks, [0] + [m for _, m in MOVES]):
        at = (mine + more) % CLASSES * DEPTH
        cols = lax.dynamic_slice_in_dim(heads, at, DEPTH, 2)
        total = total + jnp.dot(cols.reshape(512, DEPTH), part, preferred_element_type=jnp.float32)
    total = total.reshape(2, 256, WIDE)
    updated = (stream.astype(jnp.float32) + scale * (total + bias)).astype(jnp.bfloat16)
    own, other = updated[0], lax.ppermute(updated[1], "d", OTHER_CORE)
    low = jnp.where(core == 0, own[:, :SKIP], other[:, :SKIP])
    mid = jnp.where(core == 0, own[:, SKIP:], own[:, : WIDE - SKIP])
    high = jnp.where(core == 0, other[:, WIDE - SKIP :], own[:, WIDE - SKIP :])
    return jnp.concatenate([low, mid, high], axis=1)


def solution(mesh):
    line = Mesh(mesh.devices.reshape(-1), ("d",))
    return jax.shard_map(
        body,
        mesh=line,
        in_specs=(P("d", None), P("d", None), P("d", None), P(), P()),
        out_specs=P("d", None),
        check_vma=False,
    )
```

```python
import jax
import jax.numpy as jnp
import numpy as np
from jax import lax
from jax.experimental import pallas as pl
from jax.experimental.pallas import tpu as pltpu
from jax.sharding import Mesh, PartitionSpec as P

D = 3200
INNER = 2048
TOK = 256
WIDE = 1664
SKIP = D - WIDE
Y, CORES, X, Z = 8, 2, 4, 8
CLASSES = 8
ROWS = 4
DEPTH = INNER // CLASSES
MIB = 1 << 20


def index_of(core, x, y, z):
    y, x, z = y % Y, x % X, z % Z
    return (((y // 2 * CORES + core) * 2 + y % 2) * X + x) * Z + z


def places():
    for core in range(CORES):
        for y in range(Y):
            for x in range(X):
                for z in range(Z):
                    yield core, x, y, z


def class_of(x, y, z):
    return (2 * x + y + 3 * z) % CLASSES


def class_chips():
    chips = [[] for _ in range(CLASSES)]
    for core, x, y, z in places():
        if core == 0:
            chips[class_of(x, y, z)].append((x, y, z))
    return chips


def moves(step, step1=None):
    pairs = []
    for core, x, y, z in places():
        ex, ey, ez = step1 if core and step1 else step
        pairs.append((index_of(core, x, y, z), index_of(core, x + ex, y + ey, z + ez)))
    return pairs


CHIPS = class_chips()
GROUPS = [[index_of(core, *chip) for chip in chips] for core in range(CORES) for chips in CHIPS]
CHIP_PAIRS = [[index_of(0, x, y, z), index_of(1, x, y, z)] for core, x, y, z in places() if core == 0]
OTHER_CORE = [(index_of(c, x, y, z), index_of(1 - c, x, y, z)) for c, x, y, z in places()]
ORDER = np.array(
    [
        index_of(core, *chip) * ROWS + i
        for chips in CHIPS
        for chip in chips
        for core in range(CORES)
        for i in range(ROWS)
    ],
    np.int32,
)
STEPS = [
    ((1, 0, 0), None),
    ((-1, 0, 0), None),
    ((0, 1, 0), None),
    ((0, -1, 0), None),
    ((0, 0, 1), None),
    ((0, 0, -1), None),
    ((0, 1, 1), (0, -1, -1)),
]


def multiply(n, first_ref, *refs):
    pass


def early_kernel(n, rank_ref, heads_ref, *refs):
    total = None
    for k in range(n):
        part = jnp.dot(heads_ref[rank_ref[k]], refs[k][...], preferred_element_type=jnp.float32)
        total = part if total is None else total + part
    refs[n][...] = total


def late_kernel(n, rank_ref, heads_ref, early_ref, stream_ref, scale_ref, bias_ref, *refs):
    total = early_ref[...]
    for k in range(n):
        total = total + jnp.dot(heads_ref[rank_ref[k]], refs[k][...], preferred_element_type=jnp.float32)
    branch = scale_ref[...] * (total + bias_ref[...])
    refs[n][...] = (stream_ref[...].astype(jnp.float32) + branch).astype(jnp.bfloat16)


def join_kernel(core_ref, own_ref, other_ref, out_ref):
    @pl.when(core_ref[0] == 0)
    def _():
        out_ref[:, :WIDE] = own_ref[...]
        out_ref[:, WIDE:] = other_ref[:, WIDE - SKIP :]

    @pl.when(core_ref[0] == 1)
    def _():
        out_ref[:, :SKIP] = other_ref[:, :SKIP]
        out_ref[:, SKIP:] = own_ref[...]


def whole(shape):
    return pl.BlockSpec(shape, lambda i, *_: (0,) * len(shape))


PARTS = 4


def early(ranks, heads, blocks):
    n = len(blocks)
    rows = heads.shape[1]
    tile = rows // PARTS
    return pl.pallas_call(
        lambda *refs: early_kernel(n, *refs),
        grid_spec=pltpu.PrefetchScalarGridSpec(
            num_scalar_prefetch=1,
            grid=(PARTS,),
            in_specs=[pl.BlockSpec((CLASSES, tile, DEPTH), lambda i, *_: (0, i, 0))] + [whole((DEPTH, WIDE))] * n,
            out_specs=pl.BlockSpec((tile, WIDE), lambda i, *_: (i, 0)),
        ),
        out_shape=jax.ShapeDtypeStruct((rows, WIDE), jnp.float32),
        compiler_params=pltpu.CompilerParams(vmem_limit_bytes=32 * MIB),
        cost_estimate=pl.CostEstimate(flops=2 * rows * DEPTH * WIDE * n, bytes_accessed=8 * MIB, transcendentals=0),
    )(ranks, heads, *blocks)


def late(ranks, heads, total, stream, scale, bias, blocks):
    n = len(blocks)
    rows = heads.shape[1]
    tile = rows // 2
    return pl.pallas_call(
        lambda *refs: late_kernel(n, *refs),
        grid_spec=pltpu.PrefetchScalarGridSpec(
            num_scalar_prefetch=1,
            grid=(2,),
            in_specs=[
                pl.BlockSpec((CLASSES, tile, DEPTH), lambda i, *_: (0, i, 0)),
                pl.BlockSpec((tile, WIDE), lambda i, *_: (i, 0)),
                pl.BlockSpec((tile, WIDE), lambda i, *_: (i, 0)),
                whole((1, WIDE)),
                whole((1, WIDE)),
            ]
            + [whole((DEPTH, WIDE))] * n,
            out_specs=pl.BlockSpec((tile, WIDE), lambda i, *_: (i, 0)),
        ),
        out_shape=jax.ShapeDtypeStruct((rows, WIDE), jnp.bfloat16),
        compiler_params=pltpu.CompilerParams(vmem_limit_bytes=32 * MIB),
        cost_estimate=pl.CostEstimate(flops=2 * rows * DEPTH * WIDE * n, bytes_accessed=4 * MIB, transcendentals=0),
    )(ranks, heads, total, stream, scale, bias, *blocks)


def join(core, own, other):
    tile = TOK // 2
    return pl.pallas_call(
        join_kernel,
        grid_spec=pltpu.PrefetchScalarGridSpec(
            num_scalar_prefetch=1,
            grid=(2,),
            in_specs=[pl.BlockSpec((tile, WIDE), lambda i, *_: (i, 0))] * 2,
            out_specs=pl.BlockSpec((tile, D), lambda i, *_: (i, 0)),
        ),
        out_shape=jax.ShapeDtypeStruct((TOK, D), jnp.bfloat16),
        compiler_params=pltpu.CompilerParams(vmem_limit_bytes=16 * MIB),
    )(core.reshape(1), own, other)


def body(residual, heads_out, out_weight, out_bias, layer_scale):
    me = lax.axis_index("d")
    core = me // (2 * X * Z) % CORES
    z = me % Z
    x = me // Z % X
    y = me // (CORES * 2 * X * Z) * 2 + me // (X * Z) % 2
    mine = class_of(x, y, z)
    first = core * SKIP

    chip_rows = lax.all_gather(out_weight, "d", axis=0, axis_index_groups=CHIP_PAIRS)
    chip_rows = lax.dynamic_slice_in_dim(chip_rows, first, WIDE, 2).reshape(1, CORES * ROWS, WIDE)
    for_each = jnp.broadcast_to(chip_rows, (len(CHIPS[0]), CORES * ROWS, WIDE))
    block = lax.all_to_all(for_each, "d", 0, 0, axis_index_groups=GROUPS, tiled=True).reshape(DEPTH, WIDE)

    pick = (lax.broadcasted_iota(jnp.int32, (INNER, INNER), 0) == ORDER[None, :]).astype(jnp.bfloat16)
    own_heads = jnp.dot(heads_out, pick, preferred_element_type=jnp.float32).astype(jnp.bfloat16)
    own_heads = own_heads.reshape(TOK, CLASSES, DEPTH).transpose(1, 0, 2)
    other_heads = lax.ppermute(own_heads, "d", OTHER_CORE)
    own_stream = lax.dynamic_slice_in_dim(residual, first, WIDE, 1)
    other_stream = lax.ppermute(lax.dynamic_slice_in_dim(residual, SKIP - first, WIDE, 1), "d", OTHER_CORE)
    scale = lax.dynamic_slice_in_dim(layer_scale, first, WIDE, 0).reshape(1, WIDE)
    bias = lax.dynamic_slice_in_dim(out_bias, first, WIDE, 0).reshape(1, WIDE)
    block, own_heads, other_heads, own_stream, other_stream = lax.optimization_barrier(
        (block, own_heads, other_heads, own_stream, other_stream)
    )

    blocks, ranks = [block], [mine]
    for step, step1 in STEPS:
        blocks.append(lax.ppermute(block, "d", moves(step, step1)))
        ranks.append((mine - class_of(*step)) % CLASSES)
    ranks = jnp.stack(ranks).astype(jnp.int32)

    k = ORDER_EARLY
    heads = jnp.concatenate([other_heads, own_heads], axis=1)
    total = early(ranks[:k], heads, blocks[:k])
    other = late(ranks[k:], other_heads, total[:TOK], other_stream, scale, bias, blocks[k:])
    came = lax.ppermute(other, "d", OTHER_CORE)
    own = late(ranks[k:], own_heads, total[TOK:], own_stream, scale, bias, blocks[k:])
    return join(core, own, came)


ORDER_EARLY = 5


def solution(mesh):
    line = Mesh(mesh.devices.reshape(-1), ("d",))
    return jax.shard_map(
        body,
        mesh=line,
        in_specs=(P("d", None), P("d", None), P("d", None), P(), P()),
        out_specs=P("d", None),
        check_vma=False,
    )
```

```python
import functools

import jax
import jax.numpy as jnp
import numpy as np
from jax import lax
from jax.experimental import pallas as pl
from jax.experimental.pallas import tpu as pltpu
from jax.sharding import Mesh, PartitionSpec as P

D = 3200
INNER = 2048
TOK = 256
WIDE = 1664
SKIP = D - WIDE
Y, CORES, X, Z = 8, 2, 4, 8
CLASSES = 8
ROWS = 4
DEPTH = INNER // CLASSES
MIB = 1 << 20


def index_of(core, x, y, z):
    y, x, z = y % Y, x % X, z % Z
    return (((y // 2 * CORES + core) * 2 + y % 2) * X + x) * Z + z


def places():
    for core in range(CORES):
        for y in range(Y):
            for x in range(X):
                for z in range(Z):
                    yield core, x, y, z


def class_of(x, y, z):
    return (2 * x + y + 3 * z) % CLASSES


def class_chips():
    chips = [[] for _ in range(CLASSES)]
    for core, x, y, z in places():
        if core == 0:
            chips[class_of(x, y, z)].append((x, y, z))
    return chips


def moves(step, step1=None):
    pairs = []
    for core, x, y, z in places():
        ex, ey, ez = step1 if core and step1 else step
        pairs.append((index_of(core, x, y, z), index_of(core, x + ex, y + ey, z + ez)))
    return pairs


CHIPS = class_chips()
GROUPS = [[index_of(core, *chip) for chip in chips] for core in range(CORES) for chips in CHIPS]
CHIP_PAIRS = [[index_of(0, x, y, z), index_of(1, x, y, z)] for core, x, y, z in places() if core == 0]
OTHER_CORE = [(index_of(c, x, y, z), index_of(1 - c, x, y, z)) for c, x, y, z in places()]
ORDER = np.array(
    [
        index_of(core, *chip) * ROWS + i
        for chips in CHIPS
        for chip in chips
        for core in range(CORES)
        for i in range(ROWS)
    ],
    np.int32,
)
STEPS = [
    ((1, 0, 0), (-1, 0, 0)),
    ((0, 1, 1), (0, -1, -1)),
    ((0, 1, 0), (0, -1, 0)),
    ((0, 0, 1), (0, 0, -1)),
    ((-1, 0, 0), (1, 0, 0)),
    ((0, -1, 0), (0, 1, 0)),
    ((0, 0, -1), (0, 0, 1)),
]

def fetch(block_refs, slots, sems):
    copies = [pltpu.make_async_copy(ref, slots.at[k], sems.at[k]) for k, ref in enumerate(block_refs)]
    for copy in copies:
        copy.start()
    return copies


def early_kernel(n, rank_ref, heads_ref, *refs):
    block_refs, so_far_ref, (total_ref, slots, sems) = refs[:n], refs[n:-3], refs[-3:]
    copies = fetch(block_refs, slots, sems)
    for copy in copies:
        copy.wait()
    for columns in TILES:
        total = so_far_ref[0][:, columns] if so_far_ref else 0.0
        for k in range(n):
            part = slots[k, :, columns]
            total = total + jnp.dot(heads_ref[rank_ref[k]], part, preferred_element_type=jnp.float32)
        total_ref[:, columns] = total


def late_kernel(rows, rank_ref, heads_ref, so_far_ref, stream_ref, scale_ref, bias_ref, *refs):
    *block_refs, out_ref, slots, sems = refs
    copies = fetch(block_refs, slots, sems)
    for copy in copies:
        copy.wait()
    for columns in TILES:
        total = so_far_ref[rows, columns]
        for k in range(len(copies)):
            part = slots[k, :, columns]
            total = total + jnp.dot(heads_ref[rank_ref[k], rows], part, preferred_element_type=jnp.float32)
        branch = scale_ref[:, columns] * (total + bias_ref[:, columns])
        out_ref[:, columns] = (stream_ref[:, columns].astype(jnp.float32) + branch).astype(jnp.bfloat16)


TILES = [slice(c, min(c + 512, WIDE)) for c in range(0, WIDE, 512)]
VMEM_SPEC = pl.BlockSpec(memory_space=pltpu.VMEM)
SMEM_SPEC = pl.BlockSpec(memory_space=pltpu.SMEM)
ANY_SPEC = pl.BlockSpec(memory_space=pl.ANY)


def slots_for(n):
    return [pltpu.VMEM((n, DEPTH, WIDE), jnp.bfloat16), pltpu.SemaphoreType.DMA((n,))]


def cost(n, rows):
    return pl.CostEstimate(flops=2 * rows * n * DEPTH * WIDE, bytes_accessed=n * DEPTH * WIDE * 2, transcendentals=0)


def early(ranks, heads, blocks, *so_far):
    n = len(blocks)
    return pl.pallas_call(
        functools.partial(early_kernel, n),
        in_specs=[SMEM_SPEC, VMEM_SPEC] + [ANY_SPEC] * n + [VMEM_SPEC] * len(so_far),
        out_specs=VMEM_SPEC,
        out_shape=jax.ShapeDtypeStruct((2 * TOK, WIDE), jnp.float32),
        scratch_shapes=slots_for(n),
        compiler_params=pltpu.CompilerParams(vmem_limit_bytes=24 * MIB),
        cost_estimate=cost(n, 2 * TOK),
    )(ranks, heads, *blocks, *so_far)


def late(half, ranks, heads, so_far, stream, scale, bias, blocks):
    n = len(blocks)
    return pl.pallas_call(
        functools.partial(late_kernel, slice(half * TOK, (half + 1) * TOK)),
        in_specs=[SMEM_SPEC] + [VMEM_SPEC] * 5 + [ANY_SPEC] * n,
        out_specs=VMEM_SPEC,
        out_shape=jax.ShapeDtypeStruct((TOK, WIDE), jnp.bfloat16),
        scratch_shapes=slots_for(n),
        compiler_params=pltpu.CompilerParams(vmem_limit_bytes=24 * MIB),
        cost_estimate=cost(n, TOK),
    )(ranks, heads, so_far, stream, scale, bias, *blocks)


def join_kernel(core_ref, own_ref, other_ref, out_ref):
    @pl.when(core_ref[0] == 0)
    def _():
        out_ref[:, :WIDE] = own_ref[...]
        out_ref[:, WIDE:] = other_ref[:, WIDE - SKIP :]

    @pl.when(core_ref[0] == 1)
    def _():
        out_ref[:, :SKIP] = other_ref[:, :SKIP]
        out_ref[:, SKIP:] = own_ref[...]


def join(core, own, other):
    tile = TOK // 2
    return pl.pallas_call(
        join_kernel,
        grid_spec=pltpu.PrefetchScalarGridSpec(
            num_scalar_prefetch=1,
            grid=(2,),
            in_specs=[pl.BlockSpec((tile, WIDE), lambda i, *_: (i, 0))] * 2,
            out_specs=pl.BlockSpec((tile, D), lambda i, *_: (i, 0)),
        ),
        out_shape=jax.ShapeDtypeStruct((TOK, D), jnp.bfloat16),
        compiler_params=pltpu.CompilerParams(vmem_limit_bytes=16 * MIB),
    )(core.reshape(1), own, other)


def rise(core, step, step1):
    return class_of(*step) + core * (class_of(*step1) - class_of(*step))


def body(residual, heads_out, out_weight, out_bias, layer_scale):
    me = lax.axis_index("d")
    core = me // (2 * X * Z) % CORES
    z = me % Z
    x = me // Z % X
    y = me // (CORES * 2 * X * Z) * 2 + me // (X * Z) % 2
    mine = class_of(x, y, z)
    first = core * SKIP

    chip_rows = lax.all_gather(out_weight, "d", axis=0, axis_index_groups=CHIP_PAIRS)
    chip_rows = lax.dynamic_slice_in_dim(chip_rows, first, WIDE, 2).reshape(1, CORES * ROWS, WIDE)
    for_each = jnp.broadcast_to(chip_rows, (len(CHIPS[0]), CORES * ROWS, WIDE))
    block = lax.all_to_all(for_each, "d", 0, 0, axis_index_groups=GROUPS, tiled=True).reshape(DEPTH, WIDE)

    pick = (lax.broadcasted_iota(jnp.int32, (INNER, INNER), 0) == ORDER[None, :]).astype(jnp.bfloat16)
    own_heads = jnp.dot(heads_out, pick, preferred_element_type=jnp.float32).astype(jnp.bfloat16)
    own_heads = own_heads.reshape(TOK, CLASSES, DEPTH).transpose(1, 0, 2)
    other_heads = lax.ppermute(own_heads, "d", OTHER_CORE)
    own_stream = lax.dynamic_slice_in_dim(residual, first, WIDE, 1)
    other_stream = lax.ppermute(lax.dynamic_slice_in_dim(residual, SKIP - first, WIDE, 1), "d", OTHER_CORE)
    scale = lax.dynamic_slice_in_dim(layer_scale, first, WIDE, 0).reshape(1, WIDE)
    bias = lax.dynamic_slice_in_dim(out_bias, first, WIDE, 0).reshape(1, WIDE)
    heads = jnp.concatenate([other_heads, own_heads], axis=1)
    block, heads, own_stream, other_stream = lax.optimization_barrier((block, heads, own_stream, other_stream))

    ranks = jnp.stack([mine] + [(mine - rise(core, *step)) % CLASSES for step in STEPS]).astype(jnp.int32)
    blocks = [block] + [lax.ppermute(block, "d", moves(*step)) for step in STEPS[:AHEAD]]
    total = early(ranks[:FIRST], heads, blocks[:FIRST])
    block, total = lax.optimization_barrier((block, total))
    blocks += [lax.ppermute(block, "d", moves(*step)) for step in STEPS[AHEAD:]]
    total = early(ranks[FIRST:SOON], heads, blocks[FIRST:SOON], total)
    last = (ranks[SOON:], heads, total)
    other = late(0, *last, other_stream, scale, bias, blocks[SOON:])
    came = lax.ppermute(other, "d", OTHER_CORE)
    own = late(1, *last, own_stream, scale, bias, blocks[SOON:])
    return join(core, own, came)


FIRST = 1
AHEAD = 5
SOON = 6


def solution(mesh):
    line = Mesh(mesh.devices.reshape(-1), ("d",))
    return jax.shard_map(
        body,
        mesh=line,
        in_specs=(P("d", None), P("d", None), P("d", None), P(), P()),
        out_specs=P("d", None),
        check_vma=False,
    )
```

```python
import functools

import jax
import jax.numpy as jnp
import numpy as np
from jax import lax
from jax.experimental import pallas as pl
from jax.experimental.pallas import tpu as pltpu
from jax.sharding import Mesh, PartitionSpec as P

D = 3200
INNER = 2048
TOK = 256
WIDE = 1664
SKIP = D - WIDE
Y, CORES, X, Z = 8, 2, 4, 8
CLASSES = 8
ROWS = 4
DEPTH = INNER // CLASSES
MIB = 1 << 20


def index_of(core, x, y, z):
    y, x, z = y % Y, x % X, z % Z
    return (((y // 2 * CORES + core) * 2 + y % 2) * X + x) * Z + z


def places():
    for core in range(CORES):
        for y in range(Y):
            for x in range(X):
                for z in range(Z):
                    yield core, x, y, z


def class_of(x, y, z):
    return (2 * x + y + 3 * z) % CLASSES


def class_chips():
    chips = [[] for _ in range(CLASSES)]
    for core, x, y, z in places():
        if core == 0:
            chips[class_of(x, y, z)].append((x, y, z))
    return chips


def moves(step, step1=None):
    pairs = []
    for core, x, y, z in places():
        ex, ey, ez = step1 if core and step1 else step
        pairs.append((index_of(core, x, y, z), index_of(core, x + ex, y + ey, z + ez)))
    return pairs


CHIPS = class_chips()
GROUPS = [[index_of(core, *chip) for chip in chips] for core in range(CORES) for chips in CHIPS]
CHIP_PAIRS = [[index_of(0, x, y, z), index_of(1, x, y, z)] for core, x, y, z in places() if core == 0]
OTHER_CORE = [(index_of(c, x, y, z), index_of(1 - c, x, y, z)) for c, x, y, z in places()]
ORDER = np.array(
    [
        index_of(core, *chip) * ROWS + i
        for chips in CHIPS
        for chip in chips
        for core in range(CORES)
        for i in range(ROWS)
    ],
    np.int32,
)
STEPS = [
    ((0, 1, 1), (0, -1, -1)),
    ((1, 0, 0), (-1, 0, 0)),
    ((0, 1, 0), (0, -1, 0)),
    ((0, 0, 1), (0, 0, -1)),
    ((0, -1, 0), (0, 1, 0)),
    ((0, 0, -1), (0, 0, 1)),
    ((-1, 0, 0), (1, 0, 0)),
]

def fetch(block_refs, slots, sems):
    copies = [pltpu.make_async_copy(ref, slots.at[k], sems.at[k]) for k, ref in enumerate(block_refs)]
    for copy in copies:
        copy.start()
    return copies


def own_kernel(rank_ref, heads_ref, block_ref, total_ref, slots, sems):
    fetch([block_ref], slots, sems)[0].wait()
    for columns in TILES:
        total_ref[:, columns] = jnp.dot(
            heads_ref[rank_ref[0], :TOK], slots[0, :, columns], preferred_element_type=jnp.float32
        )


def early_kernel(n, rank_ref, heads_ref, *refs):
    block_refs, (so_far_ref, total_ref, slots, sems) = refs[:n], refs[n:]
    copies = fetch(block_refs, slots, sems)
    for copy in copies:
        copy.wait()
    for columns in TILES:
        total = 0.0
        for k in range(1, n):
            part = slots[k, :, columns]
            total = total + jnp.dot(heads_ref[rank_ref[k]], part, preferred_element_type=jnp.float32)
        own = jnp.dot(heads_ref[rank_ref[0], TOK:], slots[0, :, columns], preferred_element_type=jnp.float32)
        total_ref[:TOK, columns] = total[:TOK] + so_far_ref[:, columns]
        total_ref[TOK:, columns] = total[TOK:] + own


def late_kernel(rows, rank_ref, heads_ref, so_far_ref, stream_ref, scale_ref, bias_ref, *refs):
    *block_refs, out_ref, slots, sems = refs
    copies = fetch(block_refs, slots, sems)
    for copy in copies:
        copy.wait()
    for columns in TILES:
        total = so_far_ref[rows, columns]
        for k in range(len(copies)):
            part = slots[k, :, columns]
            total = total + jnp.dot(heads_ref[rank_ref[k], rows], part, preferred_element_type=jnp.float32)
        branch = scale_ref[:, columns] * (total + bias_ref[:, columns])
        out_ref[:, columns] = (stream_ref[:, columns].astype(jnp.float32) + branch).astype(jnp.bfloat16)


TILES = [slice(c, min(c + 512, WIDE)) for c in range(0, WIDE, 512)]
VMEM_SPEC = pl.BlockSpec(memory_space=pltpu.VMEM)
SMEM_SPEC = pl.BlockSpec(memory_space=pltpu.SMEM)
ANY_SPEC = pl.BlockSpec(memory_space=pl.ANY)


def slots_for(n):
    return [pltpu.VMEM((n, DEPTH, WIDE), jnp.bfloat16), pltpu.SemaphoreType.DMA((n,))]


def cost(n, rows):
    return pl.CostEstimate(flops=2 * rows * n * DEPTH * WIDE, bytes_accessed=n * DEPTH * WIDE * 2, transcendentals=0)


def own_sum(ranks, heads, block):
    return pl.pallas_call(
        own_kernel,
        in_specs=[SMEM_SPEC, VMEM_SPEC, ANY_SPEC],
        out_specs=VMEM_SPEC,
        out_shape=jax.ShapeDtypeStruct((TOK, WIDE), jnp.float32),
        scratch_shapes=slots_for(1),
        compiler_params=pltpu.CompilerParams(vmem_limit_bytes=24 * MIB),
        cost_estimate=cost(1, TOK),
    )(ranks, heads, block)


def early(ranks, heads, blocks, so_far):
    n = len(blocks)
    return pl.pallas_call(
        functools.partial(early_kernel, n),
        in_specs=[SMEM_SPEC, VMEM_SPEC] + [ANY_SPEC] * n + [VMEM_SPEC],
        out_specs=VMEM_SPEC,
        out_shape=jax.ShapeDtypeStruct((2 * TOK, WIDE), jnp.float32),
        scratch_shapes=slots_for(n),
        compiler_params=pltpu.CompilerParams(vmem_limit_bytes=24 * MIB),
        cost_estimate=cost(n, 2 * TOK),
    )(ranks, heads, *blocks, so_far)


def late(half, ranks, heads, so_far, stream, scale, bias, blocks):
    n = len(blocks)
    return pl.pallas_call(
        functools.partial(late_kernel, slice(half * TOK, (half + 1) * TOK)),
        in_specs=[SMEM_SPEC] + [VMEM_SPEC] * 5 + [ANY_SPEC] * n,
        out_specs=VMEM_SPEC,
        out_shape=jax.ShapeDtypeStruct((TOK, WIDE), jnp.bfloat16),
        scratch_shapes=slots_for(n),
        compiler_params=pltpu.CompilerParams(vmem_limit_bytes=24 * MIB),
        cost_estimate=cost(n, TOK),
    )(ranks, heads, so_far, stream, scale, bias, *blocks)


def join_kernel(core_ref, own_ref, other_ref, out_ref):
    @pl.when(core_ref[0] == 0)
    def _():
        out_ref[:, :WIDE] = own_ref[...]
        out_ref[:, WIDE:] = other_ref[:, WIDE - SKIP :]

    @pl.when(core_ref[0] == 1)
    def _():
        out_ref[:, :SKIP] = other_ref[:, :SKIP]
        out_ref[:, SKIP:] = own_ref[...]


def join(core, own, other):
    tile = TOK // 2
    return pl.pallas_call(
        join_kernel,
        grid_spec=pltpu.PrefetchScalarGridSpec(
            num_scalar_prefetch=1,
            grid=(2,),
            in_specs=[pl.BlockSpec((tile, WIDE), lambda i, *_: (i, 0))] * 2,
            out_specs=pl.BlockSpec((tile, D), lambda i, *_: (i, 0)),
        ),
        out_shape=jax.ShapeDtypeStruct((TOK, D), jnp.bfloat16),
        compiler_params=pltpu.CompilerParams(vmem_limit_bytes=16 * MIB),
    )(core.reshape(1), own, other)


def rise(core, step, step1):
    return class_of(*step) + core * (class_of(*step1) - class_of(*step))


def body(residual, heads_out, out_weight, out_bias, layer_scale):
    me = lax.axis_index("d")
    core = me // (2 * X * Z) % CORES
    z = me % Z
    x = me // Z % X
    y = me // (CORES * 2 * X * Z) * 2 + me // (X * Z) % 2
    mine = class_of(x, y, z)
    first = core * SKIP

    chip_rows = lax.all_gather(out_weight, "d", axis=0, axis_index_groups=CHIP_PAIRS)
    chip_rows = lax.dynamic_slice_in_dim(chip_rows, first, WIDE, 2).reshape(1, CORES * ROWS, WIDE)
    for_each = jnp.broadcast_to(chip_rows, (len(CHIPS[0]), CORES * ROWS, WIDE))
    block = lax.all_to_all(for_each, "d", 0, 0, axis_index_groups=GROUPS, tiled=True).reshape(DEPTH, WIDE)

    pick = (lax.broadcasted_iota(jnp.int32, (INNER, INNER), 0) == ORDER[None, :]).astype(jnp.bfloat16)
    own_heads = jnp.dot(heads_out, pick, preferred_element_type=jnp.float32).astype(jnp.bfloat16)
    own_heads = own_heads.reshape(TOK, CLASSES, DEPTH).transpose(1, 0, 2)
    other_heads = lax.ppermute(own_heads, "d", OTHER_CORE)
    own_stream = lax.dynamic_slice_in_dim(residual, first, WIDE, 1)
    other_stream = lax.ppermute(lax.dynamic_slice_in_dim(residual, SKIP - first, WIDE, 1), "d", OTHER_CORE)
    scale = lax.dynamic_slice_in_dim(layer_scale, first, WIDE, 0).reshape(1, WIDE)
    bias = lax.dynamic_slice_in_dim(out_bias, first, WIDE, 0).reshape(1, WIDE)
    heads = jnp.concatenate([other_heads, own_heads], axis=1)
    block, heads, own_stream, other_stream = lax.optimization_barrier((block, heads, own_stream, other_stream))

    ranks = jnp.stack([mine] + [(mine - rise(core, *step)) % CLASSES for step in STEPS]).astype(jnp.int32)
    blocks = [block] + [lax.ppermute(block, "d", moves(*step)) for step in STEPS[:AHEAD]]
    total = own_sum(ranks[:1], heads, block)
    block, total = lax.optimization_barrier((block, total))
    blocks += [lax.ppermute(block, "d", moves(*step)) for step in STEPS[AHEAD:]]
    total = early(ranks[:SOON], heads, blocks[:SOON], total)
    last = (ranks[SOON:], heads, total)
    other = late(0, *last, other_stream, scale, bias, blocks[SOON:])
    came = lax.ppermute(other, "d", OTHER_CORE)
    own = late(1, *last, own_stream, scale, bias, blocks[SOON:])
    return join(core, own, came)


AHEAD = 5
SOON = 6


def solution(mesh):
    line = Mesh(mesh.devices.reshape(-1), ("d",))
    return jax.shard_map(
        body,
        mesh=line,
        in_specs=(P("d", None), P("d", None), P("d", None), P(), P()),
        out_specs=P("d", None),
        check_vma=False,
    )
```

```python
import functools

import jax
import jax.numpy as jnp
import numpy as np
from jax import lax
from jax.experimental import pallas as pl
from jax.experimental.pallas import tpu as pltpu
from jax.sharding import Mesh, PartitionSpec as P

D = 3200
INNER = 2048
TOK = 256
WIDE = 1664
SKIP = D - WIDE
Y, CORES, X, Z = 8, 2, 4, 8
CLASSES = 8
ROWS = 4
DEPTH = INNER // CLASSES
MIB = 1 << 20


def index_of(core, x, y, z):
    y, x, z = y % Y, x % X, z % Z
    return (((y // 2 * CORES + core) * 2 + y % 2) * X + x) * Z + z


def places():
    for core in range(CORES):
        for y in range(Y):
            for x in range(X):
                for z in range(Z):
                    yield core, x, y, z


def class_of(x, y, z):
    return (2 * x + y + 3 * z) % CLASSES


def class_chips():
    chips = [[] for _ in range(CLASSES)]
    for core, x, y, z in places():
        if core == 0:
            chips[class_of(x, y, z)].append((x, y, z))
    return chips


def moves(step, step1=None):
    pairs = []
    for core, x, y, z in places():
        ex, ey, ez = step1 if core and step1 else step
        pairs.append((index_of(core, x, y, z), index_of(core, x + ex, y + ey, z + ez)))
    return pairs


CHIPS = class_chips()
GROUPS = [[index_of(core, *chip) for chip in chips] for core in range(CORES) for chips in CHIPS]
CHIP_PAIRS = [[index_of(0, x, y, z), index_of(1, x, y, z)] for core, x, y, z in places() if core == 0]
OTHER_CORE = [(index_of(c, x, y, z), index_of(1 - c, x, y, z)) for c, x, y, z in places()]
ORDER = np.array(
    [
        index_of(core, *chip) * ROWS + i
        for chips in CHIPS
        for chip in chips
        for core in range(CORES)
        for i in range(ROWS)
    ],
    np.int32,
)
STEPS = [
    ((0, 1, 1), (0, -1, -1)),
    ((1, 0, 0), (-1, 0, 0)),
    ((0, 1, 0), (0, -1, 0)),
    ((0, 0, 1), (0, 0, -1)),
    ((0, -1, 0), (0, 1, 0)),
    ((0, 0, -1), (0, 0, 1)),
    ((-1, 0, 0), (1, 0, 0)),
]

def fetch(block_refs, slots, sems):
    copies = [pltpu.make_async_copy(ref, slots.at[k], sems.at[k]) for k, ref in enumerate(block_refs)]
    for copy in copies:
        copy.start()
    return copies


def own_kernel(rank_ref, heads_ref, block_ref, total_ref, slots, sems):
    fetch([block_ref], slots, sems)[0].wait()
    for columns in TILES:
        total_ref[:, columns] = jnp.dot(
            heads_ref[rank_ref[0], :TOK], slots[0, :, columns], preferred_element_type=jnp.float32
        )


def early_kernel(n, rank_ref, heads_ref, *refs):
    block_refs, (so_far_ref, total_ref, slots, sems) = refs[:n], refs[n:]
    copies = fetch(block_refs, slots, sems)
    for copy in copies:
        copy.wait()
    for columns in TILES:
        total = 0.0
        for k in range(1, n):
            part = slots[k, :, columns]
            total = total + jnp.dot(heads_ref[rank_ref[k]], part, preferred_element_type=jnp.float32)
        own = jnp.dot(heads_ref[rank_ref[0], TOK:], slots[0, :, columns], preferred_element_type=jnp.float32)
        total_ref[:TOK, columns] = total[:TOK] + so_far_ref[:, columns]
        total_ref[TOK:, columns] = total[TOK:] + own


def late_kernel(rows, rank_ref, heads_ref, so_far_ref, stream_ref, scale_ref, bias_ref, *refs):
    *block_refs, out_ref, slots, sems = refs
    copies = fetch(block_refs, slots, sems)
    for copy in copies:
        copy.wait()
    for columns in TILES:
        total = so_far_ref[rows, columns]
        for k in range(len(copies)):
            part = slots[k, :, columns]
            total = total + jnp.dot(heads_ref[rank_ref[k], rows], part, preferred_element_type=jnp.float32)
        branch = scale_ref[:, columns] * (total + bias_ref[:, columns])
        out_ref[:, columns] = (stream_ref[:, columns].astype(jnp.float32) + branch).astype(jnp.bfloat16)


TILES = [slice(c, min(c + 512, WIDE)) for c in range(0, WIDE, 512)]
VMEM_SPEC = pl.BlockSpec(memory_space=pltpu.VMEM)
SMEM_SPEC = pl.BlockSpec(memory_space=pltpu.SMEM)
ANY_SPEC = pl.BlockSpec(memory_space=pl.ANY)


def slots_for(n):
    return [pltpu.VMEM((n, DEPTH, WIDE), jnp.bfloat16), pltpu.SemaphoreType.DMA((n,))]


def cost(n, rows):
    return pl.CostEstimate(flops=2 * rows * n * DEPTH * WIDE, bytes_accessed=n * DEPTH * WIDE * 2, transcendentals=0)


def own_sum(ranks, heads, block):
    return pl.pallas_call(
        own_kernel,
        in_specs=[SMEM_SPEC, VMEM_SPEC, ANY_SPEC],
        out_specs=VMEM_SPEC,
        out_shape=jax.ShapeDtypeStruct((TOK, WIDE), jnp.float32),
        scratch_shapes=slots_for(1),
        compiler_params=pltpu.CompilerParams(vmem_limit_bytes=24 * MIB),
        cost_estimate=cost(1, TOK),
    )(ranks, heads, block)


def early(ranks, heads, blocks, so_far):
    n = len(blocks)
    return pl.pallas_call(
        functools.partial(early_kernel, n),
        in_specs=[SMEM_SPEC, VMEM_SPEC] + [ANY_SPEC] * n + [VMEM_SPEC],
        out_specs=VMEM_SPEC,
        out_shape=jax.ShapeDtypeStruct((2 * TOK, WIDE), jnp.float32),
        scratch_shapes=slots_for(n),
        compiler_params=pltpu.CompilerParams(vmem_limit_bytes=24 * MIB),
        cost_estimate=cost(n, 2 * TOK),
    )(ranks, heads, *blocks, so_far)


def late(half, ranks, heads, so_far, stream, scale, bias, blocks):
    n = len(blocks)
    return pl.pallas_call(
        functools.partial(late_kernel, slice(half * TOK, (half + 1) * TOK)),
        in_specs=[SMEM_SPEC] + [VMEM_SPEC] * 5 + [ANY_SPEC] * n,
        out_specs=VMEM_SPEC,
        out_shape=jax.ShapeDtypeStruct((TOK, WIDE), jnp.bfloat16),
        scratch_shapes=slots_for(n),
        compiler_params=pltpu.CompilerParams(vmem_limit_bytes=24 * MIB),
        cost_estimate=cost(n, TOK),
    )(ranks, heads, so_far, stream, scale, bias, *blocks)


def join_kernel(core_ref, own_ref, other_ref, out_ref):
    @pl.when(core_ref[0] == 0)
    def _():
        out_ref[:, :WIDE] = own_ref[...]
        out_ref[:, WIDE:] = other_ref[:, WIDE - SKIP :]

    @pl.when(core_ref[0] == 1)
    def _():
        out_ref[:, :SKIP] = other_ref[:, :SKIP]
        out_ref[:, SKIP:] = own_ref[...]


def join(core, own, other):
    tile = TOK // 2
    return pl.pallas_call(
        join_kernel,
        grid_spec=pltpu.PrefetchScalarGridSpec(
            num_scalar_prefetch=1,
            grid=(2,),
            in_specs=[pl.BlockSpec((tile, WIDE), lambda i, *_: (i, 0))] * 2,
            out_specs=pl.BlockSpec((tile, D), lambda i, *_: (i, 0)),
        ),
        out_shape=jax.ShapeDtypeStruct((TOK, D), jnp.bfloat16),
        compiler_params=pltpu.CompilerParams(vmem_limit_bytes=16 * MIB),
    )(core.reshape(1), own, other)


def rise(core, step, step1):
    return class_of(*step) + core * (class_of(*step1) - class_of(*step))


def body(residual, heads_out, out_weight, out_bias, layer_scale):
    me = lax.axis_index("d")
    core = me // (2 * X * Z) % CORES
    z = me % Z
    x = me // Z % X
    y = me // (CORES * 2 * X * Z) * 2 + me // (X * Z) % 2
    mine = class_of(x, y, z)
    first = core * SKIP

    chip_rows = lax.all_gather(out_weight, "d", axis=0, axis_index_groups=CHIP_PAIRS)
    chip_rows = lax.dynamic_slice_in_dim(chip_rows, first, WIDE, 2).reshape(1, CORES * ROWS, WIDE)
    for_each = jnp.broadcast_to(chip_rows, (len(CHIPS[0]), CORES * ROWS, WIDE))
    block = lax.all_to_all(for_each, "d", 0, 0, axis_index_groups=GROUPS, tiled=True).reshape(DEPTH, WIDE)

    pick = (lax.broadcasted_iota(jnp.int32, (INNER, INNER), 0) == ORDER[None, :]).astype(jnp.bfloat16)
    own_heads = jnp.dot(heads_out, pick, preferred_element_type=jnp.float32).astype(jnp.bfloat16)
    own_heads = own_heads.reshape(TOK, CLASSES, DEPTH).transpose(1, 0, 2)
    other_heads = lax.ppermute(own_heads, "d", OTHER_CORE)
    own_stream = lax.dynamic_slice_in_dim(residual, first, WIDE, 1)
    other_stream = lax.ppermute(lax.dynamic_slice_in_dim(residual, SKIP - first, WIDE, 1), "d", OTHER_CORE)
    scale = lax.dynamic_slice_in_dim(layer_scale, first, WIDE, 0).reshape(1, WIDE)
    bias = lax.dynamic_slice_in_dim(out_bias, first, WIDE, 0).reshape(1, WIDE)
    heads = jnp.concatenate([other_heads, own_heads], axis=1)
    block, heads, own_stream, other_stream = lax.optimization_barrier((block, heads, own_stream, other_stream))

    ranks = jnp.stack([mine] + [(mine - rise(core, *step)) % CLASSES for step in STEPS]).astype(jnp.int32)
    blocks = [block] + [lax.ppermute(block, "d", moves(*step)) for step in STEPS[:AHEAD]]
    total = own_sum(ranks[:1], heads, block)
    block, total = lax.optimization_barrier((block, total))
    blocks += [lax.ppermute(block, "d", moves(*step)) for step in STEPS[AHEAD:]]
    total = early(ranks[:SOON], heads, blocks[:SOON], total)
    last = (ranks[SOON:], heads, total)
    other = late(0, *last, other_stream, scale, bias, blocks[SOON:])
    came = lax.ppermute(other, "d", OTHER_CORE)
    own = late(1, *last, own_stream, scale, bias, blocks[SOON:])
    return join(core, own, came)


AHEAD = 5
SOON = 5


def solution(mesh):
    line = Mesh(mesh.devices.reshape(-1), ("d",))
    return jax.shard_map(
        body,
        mesh=line,
        in_specs=(P("d", None), P("d", None), P("d", None), P(), P()),
        out_specs=P("d", None),
        check_vma=False,
    )
```
